32 devices in a mesh: field: 4 (over y, x), shard: 8 (over z, core).
Axes of the slice: x: 2, y: 2, z: 4, core: 2. Of those that a mesh axis runs over, the one named last changes fastest.
Arguments:
- focal_uv: float32 [512, 6, 2, 128], P(('field', 'shard')), may hold values from -1 to 1
- offsets: float32 [512, 6, 2, 128], P(('field', 'shard')), may hold values from -6 to 6
- w_diag: float32 [512, 6, 2, 128], P(('field', 'shard')), may hold values from 0.5 to 8
- w_corr: float32 [512, 6, 128], P(('field', 'shard')), may hold values from -0.6 to 0.6
- star_count: int32 [512], P(('field', 'shard')), may hold values from 16 to 128
- exposure_ids: int32 [512, 6], P(('field', 'shard')), may hold values from 0 to 4095, as said below
- ccd_ids: int32 [512, 6], P(('field', 'shard')), may hold values from 0 to 188
- exp_slot: int32 [4096], replicated, may hold values from 0 to 4095, as said below
Outputs:
- star_update: float32 [512, 2, 128], P(('field', 'shard'))
- exposure_update: float32 [56, 4096], P(None, ('field', 'shard'))
- ccd_update: float32 [189, 6], replicated
The draws below stay inside these ranges and needn't reach their ends.
Inputs may be any that keep to these rules, and one draw needn't show every extreme that they name: `exposure_ids`: exposure e belongs to owner (exp_slot[e] // 128) % 8 and field block exp_slot[e] // 1024. Among the 96 tile visits of one device (aligned blocks of 16 tiles), at most 16 have exposures of one owner, and exactly 16 for half of the owners; at most 8 have exposures of one owner in one field block, and exactly 8 for some pairs. `exp_slot`: A permutation.
All inputs are finite; a program needn't handle non-finite values.
Results may differ from the reference program's by a relative error of at most 0.0003.
Values sent between devices are 32-bit elements; how exact they have to be, the bound alone decides.
A program may use at most 256 MiB of HBM per device.

```python
import math
import jax
import jax.numpy as jnp
import numpy as np
from jax import lax

ORDER = 6
POLY = 28
STARS = 128
VISITS = 6
NCCD = 189
TILES_DEV = 16
EXP_DEV = 128
TILES = 512
EXPOSURES = 4096
CAP = 16
N_FIELD = 4
N_SHARD = 8


def owner_layout(key):
    return jax.random.permutation(jax.random.fold_in(key, 17), EXPOSURES).astype(jnp.int32)


def draw_exp_slot(key, part):
    return owner_layout(key)


def draw_exposure_ids(key, part):
    slot_of = owner_layout(key)
    inverse = jnp.zeros((EXPOSURES,), jnp.int32).at[slot_of].set(jnp.arange(EXPOSURES, dtype=jnp.int32))
    ranks = np.concatenate([np.repeat(np.arange(N_SHARD // 2), CAP), np.repeat(np.arange(N_SHARD // 2, N_SHARD), CAP // 2)]).astype(np.int32)
    devices_all = N_FIELD * N_SHARD
    visits_dev = TILES_DEV * VISITS
    field_keys = jax.random.split(jax.random.fold_in(key, 23), N_FIELD)
    orders = jax.vmap(lambda single: jax.random.permutation(single, N_SHARD))(field_keys).astype(jnp.int32)
    device_keys = jax.random.split(jax.random.fold_in(key, 29), devices_all)
    field_of = jnp.arange(devices_all, dtype=jnp.int32) // N_SHARD

    def arrange(single, field_index):
        return jax.random.permutation(single, orders[field_index][jnp.asarray(ranks)])
    owners = jax.vmap(arrange)(device_keys, field_of).astype(jnp.int32)
    marks = (owners[:, :, None] == jnp.arange(N_SHARD, dtype=jnp.int32)[None, None, :]).astype(jnp.int32)
    seen = jnp.cumsum(marks, axis=1) - marks
    rank_in = jnp.sum(seen * marks, axis=2)
    counts = jnp.sum(marks, axis=1)
    full = jnp.take_along_axis(counts, owners, axis=1) == CAP
    first = jax.random.randint(jax.random.fold_in(key, 41), (devices_all, N_SHARD), 0, N_FIELD)
    second = (first + jax.random.randint(jax.random.fold_in(key, 43), (devices_all, N_SHARD), 1, N_FIELD)) % N_FIELD
    first_of = jnp.take_along_axis(first, owners, axis=1)
    second_of = jnp.take_along_axis(second, owners, axis=1)
    loose = jax.random.randint(jax.random.fold_in(key, 31), (devices_all, visits_dev), 0, N_FIELD)
    fblock = jnp.where(full, jnp.where(rank_in < CAP // 2, first_of, second_of), loose)
    within = jax.random.randint(jax.random.fold_in(key, 37), (devices_all, visits_dev), 0, EXP_DEV)
    position = (fblock * N_SHARD + owners) * EXP_DEV + within
    return inverse[position].reshape(TILES, VISITS).astype(jnp.int32)


def place_ends(values, rng, least, high):
    longest = values.shape.index(max(values.shape))
    spots = []
    for shift in (0, 1):
        where = [jax.random.randint(jax.random.fold_in(rng, axis), (), 0, length) for axis, length in enumerate(values.shape)]
        where[longest] = (where[longest] + shift) % values.shape[longest]
        spots.append(tuple(where))
    return values.at[spots[0]].set(least).at[spots[1]].set(high)


def steps_of(rng, dims, cuts, least, top_value):
    def one(axis_at, parts):
        draws = jax.random.uniform(jax.random.fold_in(jax.random.fold_in(rng, 6), axis_at), (parts,), jnp.float32, least / len(cuts), top_value / len(cuts))
        return jnp.repeat(jnp.exp(draws), dims[axis_at] // parts).reshape((-1,) + (1,) * (len(dims) - axis_at - 1))

    loudness = one(*cuts[0])
    for cut in cuts[1:]:
        loudness = loudness * one(*cut)
    return loudness


def gaussian(key, dims, scale, most, cuts=(), held_as=jnp.bfloat16):
    values = scale * jax.random.normal(key, dims, jnp.float32)
    if cuts:
        values = values * steps_of(key, dims, cuts, -0.22, 0.18)
    return jnp.clip(values, -most, most).astype(held_as)


def setup_inputs(seed: int = 0) -> dict:
    seeds = jax.random.split(jax.random.key(seed), 9)
    return {
        "focal_uv": jnp.clip(jax.random.uniform(seeds[0], (TILES, VISITS, 2, STARS), jnp.float32, -1.0, 1.0) * steps_of(seeds[0], (TILES, VISITS, 2, STARS), ((0, 32),), -0.4, 0.0), -1.0, 1.0),
        "offsets": gaussian(seeds[1], (TILES, VISITS, 2, STARS), 1.0, 6.0, ((0, 32),), jnp.float32),
        "w_diag": jnp.clip(jnp.exp(math.log(8.0) - 2.7725887 * jax.random.uniform(seeds[2], (TILES, VISITS, 2, STARS), jnp.float32) ** steps_of(seeds[2], (TILES, VISITS, 2, STARS), ((0, 32),), -0.2, 0.2)), 0.5, 8.0),
        "w_corr": jnp.clip(jax.random.uniform(seeds[3], (TILES, VISITS, STARS), jnp.float32, -0.6, 0.6) * steps_of(seeds[3], (TILES, VISITS, STARS), ((0, 32),), -0.4, 0.0), -0.6, 0.6),
        "star_count": place_ends(jax.random.randint(seeds[4], (TILES,), 16, STARS + 1), jax.random.fold_in(seeds[4], 1), 16, STARS).astype(jnp.int32),
        "exposure_ids": draw_exposure_ids(jax.random.fold_in(seeds[8], 71), 0),
        "ccd_ids": place_ends(jax.random.randint(seeds[6], (TILES, VISITS), 0, NCCD), jax.random.fold_in(seeds[6], 1), 0, NCCD - 1).astype(jnp.int32),
        "exp_slot": draw_exp_slot(jax.random.fold_in(seeds[8], 71), 0),
    }


STAR_DAMP = 0.1
EXPOSURE_DAMP = 1.0
DETECTOR_DAMP = 1.0
HIGH = lax.Precision.HIGHEST

def legendre_terms(coord_u, coord_v):

    def series(value):
        values = [jnp.ones_like(value), value]
        for degree in range(1, ORDER):
            values.append(((2 * degree + 1) * value * values[degree] - degree * values[degree - 1]) / (degree + 1))
        return values
    series_u = series(coord_u)
    series_v = series(coord_v)
    terms = []
    for total in range(ORDER + 1):
        for first in range(total + 1):
            second = total - first
            terms.append(math.sqrt((2 * first + 1) * (2 * second + 1)) * series_u[first] * series_v[second])
    return jnp.stack(terms, axis=-2)

def plane_terms(coord_u, coord_v):
    return jnp.stack([jnp.ones_like(coord_u), coord_u, coord_v], axis=-2)

def star_terms(offsets, w_diag, w_corr, star_count):
    stars = offsets.shape[-1]
    present = (jnp.arange(stars, dtype=jnp.int32)[None, :] < star_count[:, None]).astype(jnp.float32)[:, None, :]
    weight_xx = w_diag[:, :, 0] * present
    weight_yy = w_diag[:, :, 1] * present
    weight_xy = w_corr * jnp.sqrt(w_diag[:, :, 0] * w_diag[:, :, 1]) * present
    resid_x = offsets[:, :, 0]
    resid_y = offsets[:, :, 1]
    hess_xx = lax.optimization_barrier(jnp.sum(weight_xx, 1)) + STAR_DAMP
    hess_yy = lax.optimization_barrier(jnp.sum(weight_yy, 1)) + STAR_DAMP
    hess_xy = lax.optimization_barrier(jnp.sum(weight_xy, 1))
    determ = hess_xx * hess_yy - hess_xy * hess_xy
    inv_xx = (hess_yy / determ)[:, None]
    inv_yy = (hess_xx / determ)[:, None]
    inv_xy = (-hess_xy / determ)[:, None]
    grad_x = lax.optimization_barrier(jnp.sum(weight_xx * resid_x + weight_xy * resid_y, 1))[:, None]
    grad_y = lax.optimization_barrier(jnp.sum(weight_xy * resid_x + weight_yy * resid_y, 1))[:, None]
    left_x = resid_x - (inv_xx * grad_x + inv_xy * grad_y)
    left_y = resid_y - (inv_xy * grad_x + inv_yy * grad_y)
    pull_x = weight_xx * left_x + weight_xy * left_y
    pull_y = weight_xy * left_x + weight_yy * left_y
    prod_11 = inv_xx * weight_xx + inv_xy * weight_xy
    prod_12 = inv_xx * weight_xy + inv_xy * weight_yy
    prod_21 = inv_xy * weight_xx + inv_yy * weight_xy
    prod_22 = inv_xy * weight_xy + inv_yy * weight_yy
    schur_xx = weight_xx - (weight_xx * prod_11 + weight_xy * prod_21)
    schur_yy = weight_yy - (weight_xy * prod_12 + weight_yy * prod_22)
    schur_xy = weight_xy - (weight_xx * prod_12 + weight_xy * prod_22)
    return ((inv_xx, inv_yy, inv_xy), (weight_xx, weight_yy, weight_xy), (schur_xx, schur_yy, schur_xy, pull_x, pull_y))

def normal_vectors(basis, schur_xx, schur_yy, schur_xy, pull_x, pull_y):

    def outer(scale):
        product = jnp.einsum('...ps,...qs->...pq', basis * scale[..., None, :], basis, precision=HIGH)
        return product.reshape(scale.shape[:-1] + (-1,))
    grad_x = jnp.einsum('...ps,...s->...p', basis, pull_x, precision=HIGH)
    grad_y = jnp.einsum('...ps,...s->...p', basis, pull_y, precision=HIGH)
    return jnp.concatenate([outer(schur_xx), outer(schur_yy), outer(schur_xy), grad_x, grad_y], axis=-1)

def batched_cholesky_solve(matrix, rhs):
    order_n = matrix.shape[0]
    rows_idx = jnp.arange(order_n, dtype=jnp.int32)
    work = matrix
    columns = []
    for step in range(order_n):
        pivot = jnp.sqrt(work[step, step])
        column = work[:, step] / pivot[None, :]
        column = jnp.where((rows_idx >= step)[:, None], column, jnp.float32(0.0))
        columns.append(column)
        work = work - column[:, None, :] * column[None, :, :]
    lower = jnp.stack(columns, axis=1)
    remain = rhs
    forward = []
    for step in range(order_n):
        value = remain[step] / lower[step, step]
        forward.append(value)
        remain = remain - lower[:, step] * value[None, :]
    remain = jnp.stack(forward, axis=0)
    backward = [None] * order_n
    for step in range(order_n - 1, -1, -1):
        value = remain[step] / lower[step, step]
        backward[step] = value
        remain = remain - lower[step] * value[None, :]
    return jnp.stack(backward, axis=0)

def solve_blocks(vectors, width, damping):
    square = width * width
    flipped = vectors.T
    count = vectors.shape[0]
    part_xx = flipped[:square].reshape(width, width, count)
    part_yy = flipped[square:2 * square].reshape(width, width, count)
    part_xy = flipped[2 * square:3 * square].reshape(width, width, count)
    matrix = jnp.concatenate([jnp.concatenate([part_xx, part_xy], 1), jnp.concatenate([part_xy, part_yy], 1)], 0)
    matrix = matrix + damping * jnp.eye(2 * width, dtype=jnp.float32)[:, :, None]
    rhs = flipped[3 * square:3 * square + 2 * width]
    return batched_cholesky_solve(matrix, rhs).T

def star_solve(inverse, weights, offsets, model_x, model_y):
    inv_xx, inv_yy, inv_xy = inverse
    weight_xx, weight_yy, weight_xy = weights
    left_x = offsets[:, :, 0] - model_x
    left_y = offsets[:, :, 1] - model_y
    grad_x = lax.optimization_barrier(jnp.sum(weight_xx * left_x + weight_xy * left_y, 1))
    grad_y = lax.optimization_barrier(jnp.sum(weight_xy * left_x + weight_yy * left_y, 1))
    return jnp.stack([inv_xx[:, 0] * grad_x + inv_xy[:, 0] * grad_y, inv_xy[:, 0] * grad_x + inv_yy[:, 0] * grad_y], axis=1)

def reference(focal_uv, offsets, w_diag, w_corr, star_count, exposure_ids, ccd_ids, exp_slot):
    tiles = offsets.shape[0]
    block = math.gcd(tiles, 256)
    count_blocks = tiles // block
    width_exp = 3 * POLY * POLY + 2 * POLY
    width_ccd = 33

    def split_blocks(array):
        return array.reshape((count_blocks, block) + array.shape[1:])
    inputs = tuple((split_blocks(array) for array in (focal_uv, offsets, w_diag, w_corr, star_count, exposure_ids, ccd_ids)))

    def accumulate(carry, item):
        exp_table, ccd_table = carry
        coords, offs, diag, corr, count, exp_ids, det_ids = item
        terms = star_terms(offs, diag, corr, count)
        basis = legendre_terms(coords[:, :, 0], coords[:, :, 1])
        plane = plane_terms(coords[:, :, 0], coords[:, :, 1])
        exp_vec = normal_vectors(basis, *terms[2]).reshape(-1, width_exp)
        ccd_vec = normal_vectors(plane, *terms[2]).reshape(-1, width_ccd)
        exp_table = exp_table + jax.ops.segment_sum(exp_vec, exp_ids.reshape(-1), num_segments=EXPOSURES)
        ccd_table = ccd_table + jax.ops.segment_sum(ccd_vec, det_ids.reshape(-1), num_segments=NCCD)
        return ((exp_table, ccd_table), None)
    start = (jnp.zeros((EXPOSURES, width_exp), jnp.float32), jnp.zeros((NCCD, width_ccd), jnp.float32))
    (exp_table, ccd_table), _ = lax.scan(accumulate, start, inputs)
    exp_solution = solve_blocks(exp_table, POLY, EXPOSURE_DAMP)
    ccd_update = solve_blocks(ccd_table, 3, DETECTOR_DAMP)
    exposure_update = jnp.zeros((2 * POLY, EXPOSURES), jnp.float32).at[:, exp_slot].set(exp_solution.T)

    def star_block(item):
        coords, offs, diag, corr, count, exp_ids, det_ids = item
        terms = star_terms(offs, diag, corr, count)
        basis = legendre_terms(coords[:, :, 0], coords[:, :, 1])
        plane = plane_terms(coords[:, :, 0], coords[:, :, 1])
        coeff = exp_solution[exp_ids]
        det_coeff = ccd_update[det_ids]
        model_x = jnp.einsum('tkp,tkps->tks', coeff[..., :POLY], basis, precision=HIGH) + jnp.einsum('tkp,tkps->tks', det_coeff[..., :3], plane, precision=HIGH)
        model_y = jnp.einsum('tkp,tkps->tks', coeff[..., POLY:], basis, precision=HIGH) + jnp.einsum('tkp,tkps->tks', det_coeff[..., 3:], plane, precision=HIGH)
        return star_solve(terms[0], terms[1], offs, model_x, model_y)
    star_update = lax.map(star_block, inputs).reshape(tiles, 2, offsets.shape[-1])
    return (star_update, exposure_update, ccd_update)
```

```python
import functools
import math

import jax
import jax.numpy as jnp
import numpy as np
from jax import lax
from jax.experimental import pallas as pl
from jax.experimental.pallas import tpu as pltpu
from jax.sharding import PartitionSpec as P

ORDER = 6
POLY = 28
NCCD = 189
LANES = 128
MESH = pl.DeviceIdType.MESH

STAR_DAMP = 0.1
EXPOSURE_DAMP = 1.0
DETECTOR_DAMP = 1.0

DEGREE = 2 * ORDER
BLOCK = 96
AT_GRAD = 3 * BLOCK
AT_ROW = AT_GRAD + 2 * POLY
AT_CCD = AT_ROW + 8
WIDTH = 384
AT_DET = 64
BF = jnp.bfloat16
F32 = jnp.float32

PAIRS = [(first, total - first) for total in range(ORDER + 1) for first in range(total + 1)]
MOMENTS = [(first, second) for first in range(DEGREE + 1) for second in range(DEGREE + 1 - first)]
SPOT = {pair: at for at, pair in enumerate(MOMENTS)}
CCD_MOMENTS = [(0, 0), (1, 0), (0, 1), (2, 0), (1, 1), (0, 2)]
SIZE = 2 * POLY
TILES = SIZE // 8


def base_of(row):
    return sum(TILES - r // 8 for r in range(row))


def tile_at(row, column_tile):
    return 8 * (base_of(row) + column_tile - row // 8)


def bf16_parts(values):
    parts = []
    rest = np.asarray(values, np.float32)
    for _ in range(3):
        high = rest.astype(BF)
        parts.append(high)
        rest = (rest - high.astype(np.float32)).astype(np.float32)
    return np.stack(parts)


@functools.lru_cache(maxsize=None)
def expansion():
    lin = np.zeros((ORDER + 1, ORDER + 1, DEGREE + 1))
    for i in range(ORDER + 1):
        for j in range(ORDER + 1):
            one, two = np.zeros(i + 1), np.zeros(j + 1)
            one[i], two[j] = 1.0, 1.0
            prod = np.polynomial.legendre.legmul(one, two)
            lin[i, j, : len(prod)] = prod
    pair = np.zeros((POLY, POLY, BLOCK))
    for p, (i, j) in enumerate(PAIRS):
        for q, (k, l) in enumerate(PAIRS):
            scale = math.sqrt((2 * i + 1) * (2 * j + 1) * (2 * k + 1) * (2 * l + 1))
            for at, (a, b) in enumerate(MOMENTS):
                pair[p, q, at] = scale * lin[i, k, a] * lin[j, l, b]
    top, low = [], []
    for row in range(SIZE):
        for col in range(8 * (row // 8), SIZE):
            line = np.zeros(3 * BLOCK)
            kind = row // POLY + col // POLY
            line[kind * BLOCK : (kind + 1) * BLOCK] = pair[row % POLY, col % POLY]
            if row == col:
                line[kind * BLOCK + len(MOMENTS)] = EXPOSURE_DAMP
            if row < POLY:
                top.append(line[: 2 * BLOCK])
            else:
                low.append(line[2 * BLOCK :])
    return bf16_parts(np.stack(top)), bf16_parts(np.stack(low))


def split3(x):
    high = x.astype(BF)
    rest = x - high.astype(F32)
    mid = rest.astype(BF)
    low = (rest - mid.astype(F32)).astype(BF)
    return high, mid, low


def dot(a, b):
    return jnp.dot(a, b, preferred_element_type=F32)


def dot_nt(a, b):
    return lax.dot_general(a, b, (((1,), (1,)), ((), ())), preferred_element_type=F32)


def series(value, degree_max):
    values = [jnp.ones_like(value), value]
    for degree in range(1, degree_max):
        values.append(
            (2 * degree + 1) / (degree + 1) * value * values[degree]
            - degree / (degree + 1) * values[degree - 1]
        )
    return values


def iota(shape, axis):
    return lax.broadcasted_iota(jnp.int32, shape, axis)


def star_parts(tiles, visits, off_ref, wd_ref, wc_ref, cnt_ref):
    square = iota((tiles, tiles), 0) == iota((tiles, tiles), 1)
    count = jnp.sum(jnp.where(square, cnt_ref[...].astype(F32), 0.0), axis=1, keepdims=True)
    present = (iota((tiles, LANES), 1).astype(F32) < count).astype(F32)
    weights, resid = [], []
    for k in range(visits):
        d0 = wd_ref[pl.ds(2 * k, tiles, stride=2 * visits), :]
        d1 = wd_ref[pl.ds(2 * k + 1, tiles, stride=2 * visits), :]
        corr = wc_ref[k * tiles : (k + 1) * tiles, :]
        weights.append((d0 * present, d1 * present, corr * jnp.sqrt(d0 * d1) * present))
        resid.append(
            (
                off_ref[pl.ds(2 * k, tiles, stride=2 * visits), :],
                off_ref[pl.ds(2 * k + 1, tiles, stride=2 * visits), :],
            )
        )
    hess_xx = sum(w[0] for w in weights) + STAR_DAMP
    hess_yy = sum(w[1] for w in weights) + STAR_DAMP
    hess_xy = sum(w[2] for w in weights)
    inv_det = 1.0 / (hess_xx * hess_yy - hess_xy * hess_xy)
    return weights, resid, (hess_yy * inv_det, hess_xx * inv_det, -hess_xy * inv_det)


def gradient(weights, resid):
    grad_x = sum(w[0] * r[0] + w[2] * r[1] for w, r in zip(weights, resid))
    grad_y = sum(w[2] * r[0] + w[1] * r[1] for w, r in zip(weights, resid))
    return grad_x, grad_y


def visit_row(ids, tiles, visits):
    spread = (iota((tiles, LANES), 1) % tiles == iota((tiles, LANES), 0)).astype(F32)
    rows = jnp.dot(
        ids.astype(F32), spread, precision=lax.Precision.HIGHEST, preferred_element_type=F32
    )
    keep = iota((visits, LANES), 0) == iota((visits, LANES), 1) // tiles
    return jnp.sum(jnp.where(keep, rows, 0.0), axis=0, keepdims=True)


def moments_kernel(
    tiles, visits, devices, cap, exp_local,
    uv_ref, off_ref, wd_ref, wc_ref, cnt_ref, eid_ref, cid_ref, slot_ref,
    out_ref, tgt_ref, leg_v, part,
):
    count = tiles * visits
    weights, resid, (inv_xx, inv_yy, inv_xy) = star_parts(
        tiles, visits, off_ref, wd_ref, wc_ref, cnt_ref
    )
    grad_x, grad_y = gradient(weights, resid)
    shift_x = inv_xx * grad_x + inv_xy * grad_y
    shift_y = inv_xy * grad_x + inv_yy * grad_y
    lists = [[] for _ in range(7)]
    for k in range(visits):
        wxx, wyy, wxy = weights[k]
        left_x, left_y = resid[k][0] - shift_x, resid[k][1] - shift_y
        prod_11 = inv_xx * wxx + inv_xy * wxy
        prod_12 = inv_xx * wxy + inv_xy * wyy
        prod_21 = inv_xy * wxx + inv_yy * wxy
        prod_22 = inv_xy * wxy + inv_yy * wyy
        for at, value in enumerate(
            (
                uv_ref[pl.ds(2 * k, tiles, stride=2 * visits), :],
                uv_ref[pl.ds(2 * k + 1, tiles, stride=2 * visits), :],
                wxx - (wxx * prod_11 + wxy * prod_21),
                wxy - (wxx * prod_12 + wxy * prod_22),
                wyy - (wxy * prod_12 + wyy * prod_22),
                wxx * left_x + wxy * left_y,
                wxy * left_x + wyy * left_y,
            )
        ):
            lists[at].append(value)
    pad = jnp.zeros((LANES - count, LANES), F32)
    cols = [jnp.concatenate(group + [pad], axis=0).T for group in lists]
    u, v = cols[0], cols[1]
    leg_u = series(u, DEGREE)
    for b, value in enumerate(series(v, DEGREE)):
        leg_v[b] = value

    def fold(value):
        return jnp.sum(value.reshape(LANES // 8, 8, LANES), axis=0)

    def put(row, value):
        part[8 * row : 8 * row + 8, :] = value

    zero = jnp.zeros((8, LANES), F32)
    for row in range(WIDTH):
        if row < AT_GRAD and row % BLOCK >= len(MOMENTS) or row >= AT_ROW:
            put(row, zero)
    for kind in range(3):
        weight = cols[2 + kind]
        for a in range(DEGREE + 1):
            scaled = weight * leg_u[a] if a else weight
            for b in range(DEGREE + 1 - a):
                value = scaled * leg_v[b] if b else scaled
                put(kind * BLOCK + SPOT[a, b], fold(value))
    for axis in range(2):
        pull = cols[5 + axis]
        for a in range(ORDER + 1):
            scaled = pull * leg_u[a] if a else pull
            for b in range(ORDER + 1 - a):
                value = scaled * leg_v[b] if b else scaled
                norm = math.sqrt((2 * a + 1) * (2 * b + 1))
                put(AT_GRAD + axis * POLY + PAIRS.index((a, b)), fold(value) * norm)
    vec = part[pl.ds(0, WIDTH, stride=8), :]
    for s in range(1, 8):
        vec = vec + part[pl.ds(s, WIDTH, stride=8), :]

    exp_id = visit_row(eid_ref[...], tiles, visits).astype(jnp.int32)
    ccd_id = visit_row(cid_ref[...], tiles, visits).astype(jnp.int32)
    groups = slot_ref.shape[0]
    pick = (iota((groups, LANES), 0) == exp_id // LANES).astype(F32)
    looked = lax.dot_general(
        slot_ref[...].astype(F32), pick, (((0,), (0,)), ((), ())),
        precision=lax.Precision.HIGHEST, preferred_element_type=F32,
    )
    inside = iota((LANES, LANES), 0) == exp_id % LANES
    place = jnp.sum(jnp.where(inside, looked, 0.0), axis=0, keepdims=True).astype(jnp.int32)
    valid = iota((1, LANES), 1) < count
    dest = jnp.where(valid, place // exp_local, -1)
    local_row = place % exp_local
    marks = (iota((devices, LANES), 0) == dest).astype(F32)
    before = (iota((LANES, LANES), 0) < iota((LANES, LANES), 1)).astype(BF)
    rank = jnp.sum(marks * dot(marks.astype(BF), before), axis=0, keepdims=True)
    target = jnp.where(valid, dest * cap + rank.astype(jnp.int32), -1)
    ccd_id = jnp.where(valid, ccd_id, -1)
    slots = devices * cap
    send = (iota((slots, LANES), 0) == target).astype(F32).astype(BF)
    seen = (iota((slots, LANES), 0) == ccd_id).astype(F32).astype(BF)
    tgt_ref[...] = jnp.where(iota((8, LANES), 0) == 0, target, ccd_id)

    vec = jnp.where(iota((WIDTH, LANES), 0) == AT_ROW, (local_row + 1).astype(F32), vec)
    out = sum(dot_nt(send, piece) for piece in split3(vec))
    picked = [vec[kind * BLOCK + SPOT[m] : kind * BLOCK + SPOT[m] + 1] for kind in range(3) for m in CCD_MOMENTS]
    for axis in range(2):
        for m in ((0, 0), (1, 0), (0, 1)):
            at = AT_GRAD + axis * POLY + PAIRS.index(m)
            picked.append(vec[at : at + 1])
    shift = AT_CCD - 2 * LANES
    ccd_vec = jnp.concatenate(
        [jnp.zeros((shift, LANES), F32)] + picked
        + [jnp.zeros((LANES - shift - len(picked), LANES), F32)], axis=0,
    )
    tail = out[:, 2 * LANES :] + sum(dot_nt(seen, piece) for piece in split3(ccd_vec))
    out_ref[...] = jnp.concatenate([out[:, : 2 * LANES], tail], axis=1)


def exchange_kernel(fields, shards_n, src_ref, dst_ref, send_sem, recv_sem, own_sem):
    devices = fields * shards_n
    me = lax.axis_index("field") * shards_n + lax.axis_index("shard")
    barrier = pltpu.get_barrier_semaphore()

    def greet(step, carry):
        peer = lax.rem(me + step, devices)
        pl.semaphore_signal(
            barrier, inc=1, device_id=(peer // shards_n, peer % shards_n), device_id_type=MESH
        )
        return carry

    lax.fori_loop(1, devices, greet, 0)
    own = pltpu.make_async_copy(src_ref.at[me], dst_ref.at[me], own_sem)
    own.start()
    pl.semaphore_wait(barrier, devices - 1)

    def copy(step):
        peer = lax.rem(me + step, devices)
        return pltpu.make_async_remote_copy(
            src_ref=src_ref.at[peer],
            dst_ref=dst_ref.at[me],
            send_sem=send_sem.at[step],
            recv_sem=recv_sem.at[step],
            device_id=(peer // shards_n, peer % shards_n),
            device_id_type=MESH,
        )

    def launch(step, carry):
        copy(step).start()
        return carry

    def finish(step, carry):
        copy(step).wait_send()
        origin = lax.rem(me - step + devices, devices)
        pltpu.make_async_remote_copy(
            src_ref=src_ref.at[me],
            dst_ref=dst_ref.at[origin],
            send_sem=send_sem.at[step],
            recv_sem=recv_sem.at[step],
            device_id=(origin // shards_n, origin % shards_n),
            device_id_type=MESH,
        ).wait_recv()
        return carry

    lax.fori_loop(1, devices, launch, 0)
    own.wait()
    lax.fori_loop(1, devices, finish, 0)


def exchange(values, fields, shards_n, collective_id):
    devices = fields * shards_n
    return pl.pallas_call(
        functools.partial(exchange_kernel, fields, shards_n),
        out_shape=jax.ShapeDtypeStruct(values.shape, values.dtype),
        in_specs=[pl.BlockSpec(memory_space=pltpu.VMEM)],
        out_specs=pl.BlockSpec(memory_space=pltpu.VMEM),
        scratch_shapes=[
            pltpu.SemaphoreType.DMA((devices,)),
            pltpu.SemaphoreType.DMA((devices,)),
            pltpu.SemaphoreType.DMA,
        ],
        compiler_params=pltpu.CompilerParams(collective_id=collective_id, has_side_effects=True),
    )(values)


def small_solve(matrix, rhs):
    size = len(rhs)
    work = [list(line) for line in matrix]
    rhs = list(rhs)
    inverse = []
    for k in range(size):
        inv = 1.0 / work[k][k]
        inverse.append(inv)
        for r in range(k + 1, size):
            coef = work[k][r] * inv
            for c in range(r, size):
                work[r][c] = work[r][c] - coef * work[k][c]
            rhs[r] = rhs[r] - coef * rhs[k]
    out = [None] * size
    for k in range(size - 1, -1, -1):
        value = rhs[k]
        for c in range(k + 1, size):
            value = value - work[k][c] * out[c]
        out[k] = value * inverse[k]
    return out


def solve_kernel(cap, recv_ref, top_ref, low_ref, exp_ref, back_ref, mat, coefs, dinv):
    slots = recv_ref.shape[0]
    exp_local = exp_ref.shape[1]
    recv = recv_ref[...]
    flipped = recv.T
    rows = recv[:, AT_ROW : AT_ROW + 1]
    own = ((iota((slots, exp_local), 1) + 1).astype(F32) == rows).astype(F32).astype(BF)
    det = (iota((slots, exp_local), 1) == iota((slots, exp_local), 0) % cap).astype(F32).astype(BF)
    parts = split3(flipped)
    table = sum(dot(piece[:AT_CCD], own) for piece in parts)
    ccd = sum(dot(piece[AT_CCD:], det) for piece in parts)

    row_at = iota((AT_GRAD, exp_local), 0)
    damp = (row_at == len(MOMENTS)) | (row_at == 2 * BLOCK + len(MOMENTS))
    held = split3(jnp.where(damp, 1.0, table[:AT_GRAD]))
    split_at = top_ref.shape[1]
    for source, first, last, begin in ((top_ref, 0, 2 * BLOCK, 0), (low_ref, 2 * BLOCK, 3 * BLOCK, split_at)):
        total = None
        for i, j in ((0, 2), (1, 1), (2, 0), (0, 1), (1, 0), (0, 0)):
            term = dot(source[i], held[j][first:last])
            total = term if total is None else total + term
        mat[begin : begin + source.shape[1], :] = total

    sub = iota((8, exp_local), 0)
    grad = [table[AT_GRAD + 8 * t : AT_GRAD + 8 * t + 8] for t in range(TILES)]
    for kb in range(TILES):
        block = [
            [mat[tile_at(8 * kb + r, jt) : tile_at(8 * kb + r, jt) + 8, :] for jt in range(kb, TILES)]
            for r in range(8)
        ]
        for r in range(8):
            inv = 1.0 / block[r][0][r : r + 1]
            dinv[8 * kb + r : 8 * kb + r + 1, :] = inv
            scaled = [tile * inv for tile in block[r]]
            for at, tile in enumerate(scaled):
                coefs[r, 8 * (kb + at) : 8 * (kb + at) + 8, :] = tile
            for r2 in range(r + 1, 8):
                coef = scaled[0][r2 : r2 + 1]
                block[r2] = [x - coef * y for x, y in zip(block[r2], block[r])]
            step = grad[kb][r : r + 1]
            grad[kb] = grad[kb] - jnp.where(sub > r, scaled[0] * step, 0.0)
            for at in range(1, TILES - kb):
                grad[kb + at] = grad[kb + at] - scaled[at] * step
        for r in range(8):
            for at, tile in enumerate(block[r]):
                start = tile_at(8 * kb + r, kb + at)
                mat[start : start + 8, :] = tile
        for jt in range(kb + 1, TILES):
            for row in range(8 * kb + 8, 8 * jt + 8):
                start = tile_at(row, jt)
                value = mat[start : start + 8, :]
                for r in range(8):
                    value = value - coefs[r, row : row + 1, :] * block[r][jt - kb]
                mat[start : start + 8, :] = value

    answer = [None] * TILES
    for kb in range(TILES - 1, -1, -1):
        rest, inner = [], []
        for r in range(8):
            line = grad[kb][r : r + 1]
            if kb + 1 < TILES:
                total = None
                for jt in range(kb + 1, TILES):
                    start = tile_at(8 * kb + r, jt)
                    term = mat[start : start + 8, :] * answer[jt]
                    total = term if total is None else total + term
                line = line - jnp.sum(total, axis=0, keepdims=True)
            rest.append(line)
            start = tile_at(8 * kb + r, kb)
            inner.append(mat[start : start + 8, :])
        found = [None] * 8
        for r in range(7, -1, -1):
            found[r] = rest[r] * dinv[8 * kb + r : 8 * kb + r + 1, :]
            for r2 in range(r):
                rest[r2] = rest[r2] - inner[r2][r : r + 1] * found[r]
        answer[kb] = jnp.concatenate(found, axis=0)
    solved = jnp.concatenate(answer, axis=0)
    exp_ref[...] = solved

    lines = [ccd[i : i + 1] for i in range(24)]
    grams = []
    for kind in range(3):
        m00, m10, m01, m20, m11, m02 = lines[6 * kind : 6 * kind + 6]
        uu = (2.0 * m20 + m00) * (1.0 / 3.0)
        vv = (2.0 * m02 + m00) * (1.0 / 3.0)
        grams.append([[m00, m10, m01], [m10, uu, m11], [m01, m11, vv]])
    root = 1.0 / math.sqrt(3.0)
    rhs = [lines[18], lines[19] * root, lines[20] * root, lines[21], lines[22] * root, lines[23] * root]
    matrix = [
        [grams[i // 3 + j // 3][i % 3][j % 3] + (DETECTOR_DAMP if i == j else 0.0) for j in range(6)]
        for i in range(6)
    ]
    det_update = small_solve(matrix, rhs)

    exp_rows = jnp.concatenate([solved, jnp.zeros((LANES - SIZE, exp_local), F32)], axis=0)
    det_rows = jnp.concatenate(
        [jnp.zeros((AT_DET, exp_local), F32)] + det_update
        + [jnp.zeros((LANES - AT_DET - 6, exp_local), F32)], axis=0,
    )
    back = sum(dot_nt(own, piece) for piece in split3(exp_rows))
    back_ref[...] = back + sum(dot_nt(det, piece) for piece in split3(det_rows))


def stars_kernel(
    tiles, visits, uv_ref, off_ref, wd_ref, wc_ref, cnt_ref, tgt_ref, back_ref, star_ref, ccd_ref
):
    back = back_ref[...]
    slots = back.shape[0]
    ccd_ref[...] = back[:NCCD, AT_DET : AT_DET + 6]
    pieces = split3(back)

    def take(row):
        wide = jnp.broadcast_to(tgt_ref[row : row + 1, :].astype(F32), (LANES, LANES)).T
        wide = jnp.concatenate([wide] * (slots // LANES), axis=1)
        chosen = (iota((LANES, slots), 1).astype(F32) == wide).astype(F32).astype(BF)
        return sum(dot(chosen, piece) for piece in pieces)

    exp_coef = take(0)
    det_coef = take(1)
    weights, resid, (inv_xx, inv_yy, inv_xy) = star_parts(
        tiles, visits, off_ref, wd_ref, wc_ref, cnt_ref
    )
    root = 1.0 / math.sqrt(3.0)
    moved = []
    for k in range(visits):
        u = uv_ref[pl.ds(2 * k, tiles, stride=2 * visits), :]
        v = uv_ref[pl.ds(2 * k + 1, tiles, stride=2 * visits), :]
        leg_u = [x * math.sqrt(2 * n + 1) for n, x in enumerate(series(u, ORDER))]
        leg_v = [x * math.sqrt(2 * n + 1) for n, x in enumerate(series(v, ORDER))]
        lines = slice(k * tiles, (k + 1) * tiles)
        model = []
        for axis in range(2):
            extra = {(0, 0): (0, 1.0), (1, 0): (1, root), (0, 1): (2, root)}
            total = None
            for a in range(ORDER + 1):
                inner = None
                for b in range(ORDER + 1 - a):
                    at = axis * POLY + PAIRS.index((a, b))
                    coef = exp_coef[lines, at : at + 1]
                    if (a, b) in extra:
                        where, scale = extra[a, b]
                        where += AT_DET + 3 * axis
                        coef = coef + det_coef[lines, where : where + 1] * scale
                    term = coef * leg_v[b] if b else jnp.broadcast_to(coef, u.shape)
                    inner = term if inner is None else inner + term
                term = leg_u[a] * inner if a else inner
                total = term if total is None else total + term
            model.append(total)
        moved.append((resid[k][0] - model[0], resid[k][1] - model[1]))
    grad_x, grad_y = gradient(weights, moved)
    star_ref[pl.ds(0, tiles, stride=2), :] = inv_xx * grad_x + inv_xy * grad_y
    star_ref[pl.ds(1, tiles, stride=2), :] = inv_xy * grad_x + inv_yy * grad_y


def plain(kernel, out_shape, scratch=()):
    return pl.pallas_call(
        kernel,
        out_shape=out_shape,
        scratch_shapes=list(scratch),
        compiler_params=pltpu.CompilerParams(vmem_limit_bytes=48 * 1024 * 1024),
    )


def shards(focal_uv, offsets, w_diag, w_corr, star_count, exposure_ids, ccd_ids, exp_slot):
    shards_n = lax.axis_size("shard")
    fields = lax.axis_size("field")
    devices = shards_n * fields
    tiles, visits, _, stars = offsets.shape
    cap = 2 * tiles * visits // (3 * shards_n)
    slots = devices * cap
    exp_local = exp_slot.shape[0] // devices
    assert slots >= NCCD and slots % LANES == 0 and tiles * visits <= LANES and stars == LANES
    sds = jax.ShapeDtypeStruct
    uv = focal_uv.reshape(tiles * visits * 2, stars)
    off = offsets.reshape(tiles * visits * 2, stars)
    wd = w_diag.reshape(tiles * visits * 2, stars)
    wc = w_corr.transpose(1, 0, 2).reshape(tiles * visits, stars)
    cnt = star_count.reshape(1, tiles)
    out, tgt = plain(
        functools.partial(moments_kernel, tiles, visits, devices, cap, exp_local),
        (sds((slots, WIDTH), F32), sds((8, LANES), jnp.int32)),
        (pltpu.VMEM((DEGREE + 1, stars, LANES), F32), pltpu.VMEM((8 * WIDTH, LANES), F32)),
    )(uv, off, wd, wc, cnt, exposure_ids.T, ccd_ids.T, exp_slot.reshape(-1, LANES))
    recv = exchange(out.reshape(devices, cap, WIDTH), fields, shards_n, 0).reshape(slots, WIDTH)
    top, low = expansion()
    exposure_update, back = plain(
        functools.partial(solve_kernel, cap),
        (sds((SIZE, exp_local), F32), sds((slots, LANES), F32)),
        (
            pltpu.VMEM((8 * base_of(SIZE), exp_local), F32),
            pltpu.VMEM((8, SIZE, exp_local), F32),
            pltpu.VMEM((SIZE, exp_local), F32),
        ),
    )(recv, jnp.asarray(top), jnp.asarray(low))
    got = exchange(back.reshape(devices, cap, LANES), fields, shards_n, 1).reshape(slots, LANES)
    star_update, ccd_update = plain(
        functools.partial(stars_kernel, tiles, visits),
        (sds((tiles * 2, stars), F32), sds((NCCD, 6), F32)),
    )(uv, off, wd, wc, cnt, tgt, got)
    return star_update.reshape(tiles, 2, stars), exposure_update, ccd_update


def solution(mesh):
    in_specs = (
        P(("field", "shard"), None, None, None),
        P(("field", "shard"), None, None, None),
        P(("field", "shard"), None, None, None),
        P(("field", "shard"), None, None),
        P(("field", "shard")),
        P(("field", "shard"), None),
        P(("field", "shard"), None),
        P(),
    )
    out_specs = (P(("field", "shard"), None, None), P(None, ("field", "shard")), P())
    return jax.shard_map(shards, mesh=mesh, in_specs=in_specs, out_specs=out_specs, check_vma=False)
```

```python
import functools
import math

import jax
import jax.numpy as jnp
import numpy as np
from jax import lax
from jax.experimental import pallas as pl
from jax.experimental.pallas import tpu as pltpu
from jax.sharding import PartitionSpec as P

ORDER = 6
POLY = 28
NCCD = 189
LANES = 128
MESH = pl.DeviceIdType.MESH

STAR_DAMP = 0.1
EXPOSURE_DAMP = 1.0
DETECTOR_DAMP = 1.0

DEGREE = 2 * ORDER
BLOCK = 96
AT_GRAD = 3 * BLOCK
AT_ROW = AT_GRAD + 2 * POLY
AT_CCD = AT_ROW + 8
WIDTH = 384
AT_DET = 64
BF = jnp.bfloat16
HBM = pl.BlockSpec(memory_space=pltpu.HBM)
F32 = jnp.float32

PAIRS = [(first, total - first) for total in range(ORDER + 1) for first in range(total + 1)]
MOMENTS = [(first, second) for first in range(DEGREE + 1) for second in range(DEGREE + 1 - first)]
SPOT = {pair: at for at, pair in enumerate(MOMENTS)}
CCD_MOMENTS = [(0, 0), (1, 0), (0, 1), (2, 0), (1, 1), (0, 2)]
SIZE = 2 * POLY
TILES = SIZE // 8


def base_of(row):
    return sum(TILES - r // 8 for r in range(row))


def tile_at(row, column_tile):
    return 8 * (base_of(row) + column_tile - row // 8)


@functools.lru_cache(maxsize=None)
def expansion():
    lin = np.zeros((ORDER + 1, ORDER + 1, DEGREE + 1))
    for i in range(ORDER + 1):
        for j in range(ORDER + 1):
            one, two = np.zeros(i + 1), np.zeros(j + 1)
            one[i], two[j] = 1.0, 1.0
            prod = np.polynomial.legendre.legmul(one, two)
            lin[i, j, : len(prod)] = prod
    pair = np.zeros((POLY, POLY, BLOCK))
    for p, (i, j) in enumerate(PAIRS):
        for q, (k, l) in enumerate(PAIRS):
            scale = math.sqrt((2 * i + 1) * (2 * j + 1) * (2 * k + 1) * (2 * l + 1))
            for at, (a, b) in enumerate(MOMENTS):
                pair[p, q, at] = scale * lin[i, k, a] * lin[j, l, b]
    top, low = [], []
    for row in range(SIZE):
        for col in range(8 * (row // 8), SIZE):
            line = np.zeros(3 * BLOCK)
            kind = row // POLY + col // POLY
            line[kind * BLOCK : (kind + 1) * BLOCK] = pair[row % POLY, col % POLY]
            if row == col:
                line[kind * BLOCK + len(MOMENTS)] = EXPOSURE_DAMP
            if row < POLY:
                top.append(line[: 2 * BLOCK])
            else:
                low.append(line[2 * BLOCK :])
    return np.stack(top).astype(np.float32), np.stack(low).astype(np.float32)


def split3(x):
    high = x.astype(BF)
    rest = x - high.astype(F32)
    mid = rest.astype(BF)
    low = (rest - mid.astype(F32)).astype(BF)
    return high, mid, low


def dot(a, b):
    return jnp.dot(a, b, preferred_element_type=F32)


def dot_nt(a, b):
    return lax.dot_general(a, b, (((1,), (1,)), ((), ())), preferred_element_type=F32)


def series(value, degree_max):
    values = [jnp.ones_like(value), value]
    for degree in range(1, degree_max):
        values.append(
            (2 * degree + 1) / (degree + 1) * value * values[degree]
            - degree / (degree + 1) * values[degree - 1]
        )
    return values


def iota(shape, axis):
    return lax.broadcasted_iota(jnp.int32, shape, axis)


def star_parts(tiles, visits, off_ref, wd_ref, wc_ref, cnt_ref):
    square = iota((tiles, tiles), 0) == iota((tiles, tiles), 1)
    count = jnp.sum(jnp.where(square, cnt_ref[...].astype(F32), 0.0), axis=1, keepdims=True)
    present = (iota((tiles, LANES), 1).astype(F32) < count).astype(F32)
    weights, resid = [], []
    for k in range(visits):
        d0 = wd_ref[pl.ds(2 * k, tiles, stride=2 * visits), :]
        d1 = wd_ref[pl.ds(2 * k + 1, tiles, stride=2 * visits), :]
        corr = wc_ref[k * tiles : (k + 1) * tiles, :]
        weights.append((d0 * present, d1 * present, corr * jnp.sqrt(d0 * d1) * present))
        resid.append(
            (
                off_ref[pl.ds(2 * k, tiles, stride=2 * visits), :],
                off_ref[pl.ds(2 * k + 1, tiles, stride=2 * visits), :],
            )
        )
    hess_xx = sum(w[0] for w in weights) + STAR_DAMP
    hess_yy = sum(w[1] for w in weights) + STAR_DAMP
    hess_xy = sum(w[2] for w in weights)
    inv_det = 1.0 / (hess_xx * hess_yy - hess_xy * hess_xy)
    return weights, resid, (hess_yy * inv_det, hess_xx * inv_det, -hess_xy * inv_det)


def gradient(weights, resid):
    grad_x = sum(w[0] * r[0] + w[2] * r[1] for w, r in zip(weights, resid))
    grad_y = sum(w[2] * r[0] + w[1] * r[1] for w, r in zip(weights, resid))
    return grad_x, grad_y


def visit_row(ids, tiles, visits):
    spread = (iota((tiles, LANES), 1) % tiles == iota((tiles, LANES), 0)).astype(F32)
    rows = jnp.dot(
        ids.astype(F32), spread, precision=lax.Precision.HIGHEST, preferred_element_type=F32
    )
    keep = iota((visits, LANES), 0) == iota((visits, LANES), 1) // tiles
    return jnp.sum(jnp.where(keep, rows, 0.0), axis=0, keepdims=True)


def moments_kernel(
    tiles, visits, devices, cap, exp_local,
    uv_any, off_any, wd_any, wc_any, cnt_any, eid_any, cid_any, slot_any,
    out_ref, tgt_ref, leg_v, part,
    uv_ref, off_ref, wd_ref, wc_ref, cnt_ref, eid_ref, cid_ref, slot_ref, sems,
):
    count = tiles * visits
    copies = [
        pltpu.make_async_copy(source, target, sems.at[at])
        for at, (source, target) in enumerate(
            (
                (wd_any, wd_ref), (off_any, off_ref), (wc_any, wc_ref), (cnt_any, cnt_ref),
                (uv_any, uv_ref), (eid_any, eid_ref), (cid_any, cid_ref), (slot_any, slot_ref),
            )
        )
    ]
    for one in copies:
        one.start()
    for one in copies:
        one.wait()
    weights, resid, (inv_xx, inv_yy, inv_xy) = star_parts(
        tiles, visits, off_ref, wd_ref, wc_ref, cnt_ref
    )
    grad_x, grad_y = gradient(weights, resid)
    shift_x = inv_xx * grad_x + inv_xy * grad_y
    shift_y = inv_xy * grad_x + inv_yy * grad_y
    lists = [[] for _ in range(7)]
    for k in range(visits):
        wxx, wyy, wxy = weights[k]
        left_x, left_y = resid[k][0] - shift_x, resid[k][1] - shift_y
        prod_11 = inv_xx * wxx + inv_xy * wxy
        prod_12 = inv_xx * wxy + inv_xy * wyy
        prod_21 = inv_xy * wxx + inv_yy * wxy
        prod_22 = inv_xy * wxy + inv_yy * wyy
        for at, value in enumerate(
            (
                uv_ref[pl.ds(2 * k, tiles, stride=2 * visits), :],
                uv_ref[pl.ds(2 * k + 1, tiles, stride=2 * visits), :],
                wxx - (wxx * prod_11 + wxy * prod_21),
                wxy - (wxx * prod_12 + wxy * prod_22),
                wyy - (wxy * prod_12 + wyy * prod_22),
                wxx * left_x + wxy * left_y,
                wxy * left_x + wyy * left_y,
            )
        ):
            lists[at].append(value)
    pad = jnp.zeros((LANES - count, LANES), F32)
    cols = [jnp.concatenate(group + [pad], axis=0).T for group in lists]
    u, v = cols[0], cols[1]
    leg_u = series(u, DEGREE)
    for b, value in enumerate(series(v, DEGREE)):
        leg_v[b] = value

    def fold(value):
        return jnp.sum(value.reshape(LANES // 8, 8, LANES), axis=0)

    def put(row, value):
        part[8 * row : 8 * row + 8, :] = value

    zero = jnp.zeros((8, LANES), F32)
    for row in range(WIDTH):
        if row < AT_GRAD and row % BLOCK >= len(MOMENTS) or row >= AT_ROW:
            put(row, zero)
    for kind in range(3):
        weight = cols[2 + kind]
        for a in range(DEGREE + 1):
            scaled = weight * leg_u[a] if a else weight
            for b in range(DEGREE + 1 - a):
                value = scaled * leg_v[b] if b else scaled
                put(kind * BLOCK + SPOT[a, b], fold(value))
    for axis in range(2):
        pull = cols[5 + axis]
        for a in range(ORDER + 1):
            scaled = pull * leg_u[a] if a else pull
            for b in range(ORDER + 1 - a):
                value = scaled * leg_v[b] if b else scaled
                norm = math.sqrt((2 * a + 1) * (2 * b + 1))
                put(AT_GRAD + axis * POLY + PAIRS.index((a, b)), fold(value) * norm)
    vec = part[pl.ds(0, WIDTH, stride=8), :]
    for s in range(1, 8):
        vec = vec + part[pl.ds(s, WIDTH, stride=8), :]

    exp_id = visit_row(eid_ref[...], tiles, visits).astype(jnp.int32)
    ccd_id = visit_row(cid_ref[...], tiles, visits).astype(jnp.int32)
    groups = slot_ref.shape[0]
    pick = (iota((groups, LANES), 0) == exp_id // LANES).astype(F32)
    looked = lax.dot_general(
        slot_ref[...].astype(F32), pick, (((0,), (0,)), ((), ())),
        precision=lax.Precision.HIGHEST, preferred_element_type=F32,
    )
    inside = iota((LANES, LANES), 0) == exp_id % LANES
    place = jnp.sum(jnp.where(inside, looked, 0.0), axis=0, keepdims=True).astype(jnp.int32)
    valid = iota((1, LANES), 1) < count
    dest = jnp.where(valid, place // exp_local, -1)
    local_row = place % exp_local
    marks = (iota((devices, LANES), 0) == dest).astype(F32)
    before = (iota((LANES, LANES), 0) < iota((LANES, LANES), 1)).astype(BF)
    rank = jnp.sum(marks * dot(marks.astype(BF), before), axis=0, keepdims=True)
    target = jnp.where(valid, dest * cap + rank.astype(jnp.int32), -1)
    ccd_id = jnp.where(valid, ccd_id, -1)
    slots = devices * cap
    send = (iota((slots, LANES), 0) == target).astype(F32).astype(BF)
    seen = (iota((slots, LANES), 0) == ccd_id).astype(F32).astype(BF)
    tgt_ref[...] = jnp.where(iota((8, LANES), 0) == 0, target, ccd_id)

    vec = jnp.where(iota((WIDTH, LANES), 0) == AT_ROW, (local_row + 1).astype(F32), vec)
    out = sum(dot_nt(send, piece) for piece in split3(vec))
    picked = [vec[kind * BLOCK + SPOT[m] : kind * BLOCK + SPOT[m] + 1] for kind in range(3) for m in CCD_MOMENTS]
    for axis in range(2):
        for m in ((0, 0), (1, 0), (0, 1)):
            at = AT_GRAD + axis * POLY + PAIRS.index(m)
            picked.append(vec[at : at + 1])
    shift = AT_CCD - 2 * LANES
    ccd_vec = jnp.concatenate(
        [jnp.zeros((shift, LANES), F32)] + picked
        + [jnp.zeros((LANES - shift - len(picked), LANES), F32)], axis=0,
    )
    tail = out[:, 2 * LANES :] + sum(dot_nt(seen, piece) for piece in split3(ccd_vec))
    out_ref[...] = jnp.concatenate([out[:, : 2 * LANES], tail], axis=1)


def exchange_kernel(fields, shards_n, src_ref, dst_ref, send_sem, recv_sem, own_sem):
    devices = fields * shards_n
    me = lax.axis_index("field") * shards_n + lax.axis_index("shard")
    barrier = pltpu.get_barrier_semaphore()

    def greet(step, carry):
        peer = lax.rem(me + step, devices)
        pl.semaphore_signal(
            barrier, inc=1, device_id=(peer // shards_n, peer % shards_n), device_id_type=MESH
        )
        return carry

    lax.fori_loop(1, devices, greet, 0)
    own = pltpu.make_async_copy(src_ref.at[me], dst_ref.at[me], own_sem)
    own.start()
    pl.semaphore_wait(barrier, devices - 1)

    def copy(step):
        peer = lax.rem(me + step, devices)
        return pltpu.make_async_remote_copy(
            src_ref=src_ref.at[peer],
            dst_ref=dst_ref.at[me],
            send_sem=send_sem.at[step],
            recv_sem=recv_sem.at[step],
            device_id=(peer // shards_n, peer % shards_n),
            device_id_type=MESH,
        )

    def launch(step, carry):
        copy(step).start()
        return carry

    def finish(step, carry):
        copy(step).wait_send()
        origin = lax.rem(me - step + devices, devices)
        pltpu.make_async_remote_copy(
            src_ref=src_ref.at[me],
            dst_ref=dst_ref.at[origin],
            send_sem=send_sem.at[step],
            recv_sem=recv_sem.at[step],
            device_id=(origin // shards_n, origin % shards_n),
            device_id_type=MESH,
        ).wait_recv()
        return carry

    lax.fori_loop(1, devices, launch, 0)
    lax.fori_loop(1, devices, finish, 0)
    own.wait()


def exchange(values, fields, shards_n, collective_id):
    devices = fields * shards_n
    return pl.pallas_call(
        functools.partial(exchange_kernel, fields, shards_n),
        out_shape=jax.ShapeDtypeStruct(values.shape, values.dtype),
        in_specs=[pl.BlockSpec(memory_space=pltpu.HBM)],
        out_specs=pl.BlockSpec(memory_space=pltpu.HBM),
        scratch_shapes=[
            pltpu.SemaphoreType.DMA((devices,)),
            pltpu.SemaphoreType.DMA((devices,)),
            pltpu.SemaphoreType.DMA,
        ],
        compiler_params=pltpu.CompilerParams(
            collective_id=collective_id, has_side_effects=True, vmem_limit_bytes=64 * 1024 * 1024
        ),
    )(values)


def small_solve(matrix, rhs):
    size = len(rhs)
    work = [list(line) for line in matrix]
    rhs = list(rhs)
    inverse = []
    for k in range(size):
        inv = 1.0 / work[k][k]
        inverse.append(inv)
        for r in range(k + 1, size):
            coef = work[k][r] * inv
            for c in range(r, size):
                work[r][c] = work[r][c] - coef * work[k][c]
            rhs[r] = rhs[r] - coef * rhs[k]
    out = [None] * size
    for k in range(size - 1, -1, -1):
        value = rhs[k]
        for c in range(k + 1, size):
            value = value - work[k][c] * out[c]
        out[k] = value * inverse[k]
    return out


def solve_kernel(
    cap, recv_any, top_any, low_any, exp_ref, back_ref,
    mat, coefs, dinv, recv_ref, top_ref, low_ref, sems,
):
    copies = [
        pltpu.make_async_copy(source, target, sems.at[at])
        for at, (source, target) in enumerate(
            ((recv_any, recv_ref), (top_any, top_ref), (low_any, low_ref))
        )
    ]
    for one in copies:
        one.start()
    copies[0].wait()
    slots = recv_ref.shape[0]
    exp_local = exp_ref.shape[1]
    recv = recv_ref[...]
    flipped = recv.T
    rows = recv[:, AT_ROW : AT_ROW + 1]
    own = ((iota((slots, exp_local), 1) + 1).astype(F32) == rows).astype(F32).astype(BF)
    det = (iota((slots, exp_local), 1) == iota((slots, exp_local), 0) % cap).astype(F32).astype(BF)
    parts = split3(flipped)
    table = sum(dot(piece[:AT_CCD], own) for piece in parts)
    ccd = sum(dot(piece[AT_CCD:], det) for piece in parts)

    row_at = iota((AT_GRAD, exp_local), 0)
    damp = (row_at == len(MOMENTS)) | (row_at == 2 * BLOCK + len(MOMENTS))
    held = split3(jnp.where(damp, 1.0, table[:AT_GRAD]))
    split_at = top_ref.shape[0]
    copies[1].wait()
    copies[2].wait()
    for source, first, last, begin in ((top_ref, 0, 2 * BLOCK, 0), (low_ref, 2 * BLOCK, 3 * BLOCK, split_at)):
        total = None
        pieces = split3(source[...])
        for i, j in ((0, 2), (1, 1), (2, 0), (0, 1), (1, 0), (0, 0)):
            term = dot(pieces[i], held[j][first:last])
            total = term if total is None else total + term
        mat[begin : begin + source.shape[0], :] = total

    sub = iota((8, exp_local), 0)
    grad = [table[AT_GRAD + 8 * t : AT_GRAD + 8 * t + 8] for t in range(TILES)]
    for kb in range(TILES):
        block = [
            [mat[tile_at(8 * kb + r, jt) : tile_at(8 * kb + r, jt) + 8, :] for jt in range(kb, TILES)]
            for r in range(8)
        ]
        for r in range(8):
            inv = 1.0 / block[r][0][r : r + 1]
            dinv[8 * kb + r : 8 * kb + r + 1, :] = inv
            scaled = [tile * inv for tile in block[r]]
            for at, tile in enumerate(scaled):
                coefs[r, 8 * (kb + at) : 8 * (kb + at) + 8, :] = tile
            for r2 in range(r + 1, 8):
                coef = scaled[0][r2 : r2 + 1]
                block[r2] = [x - coef * y for x, y in zip(block[r2], block[r])]
            step = grad[kb][r : r + 1]
            grad[kb] = grad[kb] - jnp.where(sub > r, scaled[0] * step, 0.0)
            for at in range(1, TILES - kb):
                grad[kb + at] = grad[kb + at] - scaled[at] * step
        for r in range(8):
            for at, tile in enumerate(block[r]):
                start = tile_at(8 * kb + r, kb + at)
                mat[start : start + 8, :] = tile
        for jt in range(kb + 1, TILES):
            for row in range(8 * kb + 8, 8 * jt + 8):
                start = tile_at(row, jt)
                value = mat[start : start + 8, :]
                for r in range(8):
                    value = value - coefs[r, row : row + 1, :] * block[r][jt - kb]
                mat[start : start + 8, :] = value

    answer = [None] * TILES
    for kb in range(TILES - 1, -1, -1):
        rest, inner = [], []
        for r in range(8):
            line = grad[kb][r : r + 1]
            if kb + 1 < TILES:
                total = None
                for jt in range(kb + 1, TILES):
                    start = tile_at(8 * kb + r, jt)
                    term = mat[start : start + 8, :] * answer[jt]
                    total = term if total is None else total + term
                line = line - jnp.sum(total, axis=0, keepdims=True)
            rest.append(line)
            start = tile_at(8 * kb + r, kb)
            inner.append(mat[start : start + 8, :])
        found = [None] * 8
        for r in range(7, -1, -1):
            found[r] = rest[r] * dinv[8 * kb + r : 8 * kb + r + 1, :]
            for r2 in range(r):
                rest[r2] = rest[r2] - inner[r2][r : r + 1] * found[r]
        answer[kb] = jnp.concatenate(found, axis=0)
    solved = jnp.concatenate(answer, axis=0)
    exp_ref[...] = solved

    lines = [ccd[i : i + 1] for i in range(24)]
    grams = []
    for kind in range(3):
        m00, m10, m01, m20, m11, m02 = lines[6 * kind : 6 * kind + 6]
        uu = (2.0 * m20 + m00) * (1.0 / 3.0)
        vv = (2.0 * m02 + m00) * (1.0 / 3.0)
        grams.append([[m00, m10, m01], [m10, uu, m11], [m01, m11, vv]])
    root = 1.0 / math.sqrt(3.0)
    rhs = [lines[18], lines[19] * root, lines[20] * root, lines[21], lines[22] * root, lines[23] * root]
    matrix = [
        [grams[i // 3 + j // 3][i % 3][j % 3] + (DETECTOR_DAMP if i == j else 0.0) for j in range(6)]
        for i in range(6)
    ]
    det_update = small_solve(matrix, rhs)

    exp_rows = jnp.concatenate([solved, jnp.zeros((LANES - SIZE, exp_local), F32)], axis=0)
    det_rows = jnp.concatenate(
        [jnp.zeros((AT_DET, exp_local), F32)] + det_update
        + [jnp.zeros((LANES - AT_DET - 6, exp_local), F32)], axis=0,
    )
    back = sum(dot_nt(own, piece) for piece in split3(exp_rows))
    back_ref[...] = back + sum(dot_nt(det, piece) for piece in split3(det_rows))


def stars_kernel(
    tiles, visits, *refs
):
    sources, (star_ref, ccd_ref), targets, sems = refs[:7], refs[7:9], refs[9:16], refs[16]
    uv_ref, off_ref, wd_ref, wc_ref, cnt_ref, tgt_ref, back_ref = targets
    copies = [
        pltpu.make_async_copy(source, target, sems.at[at])
        for at, (source, target) in enumerate(zip(sources, targets))
    ]
    for one in reversed(copies):
        one.start()
    for one in reversed(copies):
        one.wait()
    back = back_ref[...]
    slots = back.shape[0]
    ccd_ref[...] = back.T[AT_DET : AT_DET + 6, :NCCD]
    pieces = split3(back)

    def take(row):
        wide = jnp.broadcast_to(tgt_ref[row : row + 1, :].astype(F32), (LANES, LANES)).T
        wide = jnp.concatenate([wide] * (slots // LANES), axis=1)
        chosen = (iota((LANES, slots), 1).astype(F32) == wide).astype(F32).astype(BF)
        return sum(dot(chosen, piece) for piece in pieces)

    exp_coef = take(0)
    det_coef = take(1)
    weights, resid, (inv_xx, inv_yy, inv_xy) = star_parts(
        tiles, visits, off_ref, wd_ref, wc_ref, cnt_ref
    )
    root = 1.0 / math.sqrt(3.0)
    moved = []
    for k in range(visits):
        u = uv_ref[pl.ds(2 * k, tiles, stride=2 * visits), :]
        v = uv_ref[pl.ds(2 * k + 1, tiles, stride=2 * visits), :]
        leg_u = [x * math.sqrt(2 * n + 1) for n, x in enumerate(series(u, ORDER))]
        leg_v = [x * math.sqrt(2 * n + 1) for n, x in enumerate(series(v, ORDER))]
        lines = slice(k * tiles, (k + 1) * tiles)
        model = []
        for axis in range(2):
            extra = {(0, 0): (0, 1.0), (1, 0): (1, root), (0, 1): (2, root)}
            total = None
            for a in range(ORDER + 1):
                inner = None
                for b in range(ORDER + 1 - a):
                    at = axis * POLY + PAIRS.index((a, b))
                    coef = exp_coef[lines, at : at + 1]
                    if (a, b) in extra:
                        where, scale = extra[a, b]
                        where += AT_DET + 3 * axis
                        coef = coef + det_coef[lines, where : where + 1] * scale
                    term = coef * leg_v[b] if b else jnp.broadcast_to(coef, u.shape)
                    inner = term if inner is None else inner + term
                term = leg_u[a] * inner if a else inner
                total = term if total is None else total + term
            model.append(total)
        moved.append((resid[k][0] - model[0], resid[k][1] - model[1]))
    grad_x, grad_y = gradient(weights, moved)
    star_ref[pl.ds(0, tiles, stride=2), :] = inv_xx * grad_x + inv_xy * grad_y
    star_ref[pl.ds(1, tiles, stride=2), :] = inv_xy * grad_x + inv_yy * grad_y


def plain(kernel, out_shape, scratch=(), in_place=None):
    extra = {} if in_place is None else {"in_specs": in_place}
    return pl.pallas_call(
        kernel,
        out_shape=out_shape,
        **extra,
        scratch_shapes=list(scratch),
        compiler_params=pltpu.CompilerParams(vmem_limit_bytes=64 * 1024 * 1024),
    )


def shards(focal_uv, offsets, w_diag, w_corr, star_count, exposure_ids, ccd_ids, exp_slot):
    shards_n = lax.axis_size("shard")
    fields = lax.axis_size("field")
    devices = shards_n * fields
    tiles, visits, _, stars = offsets.shape
    cap = 2 * tiles * visits // (3 * shards_n)
    slots = devices * cap
    exp_local = exp_slot.shape[0] // devices
    assert slots >= NCCD and slots % LANES == 0 and tiles * visits <= LANES and stars == LANES
    sds = jax.ShapeDtypeStruct
    uv = focal_uv.reshape(tiles * visits * 2, stars)
    off = offsets.reshape(tiles * visits * 2, stars)
    wd = w_diag.reshape(tiles * visits * 2, stars)
    wc = w_corr.transpose(1, 0, 2).reshape(tiles * visits, stars)
    cnt = star_count.reshape(1, tiles)
    given = (uv, off, wd, wc, cnt, exposure_ids.T, ccd_ids.T, exp_slot.reshape(-1, LANES))
    out, tgt = plain(
        functools.partial(moments_kernel, tiles, visits, devices, cap, exp_local),
        (sds((slots, WIDTH), F32), sds((8, LANES), jnp.int32)),
        (pltpu.VMEM((DEGREE + 1, stars, LANES), F32), pltpu.VMEM((8 * WIDTH, LANES), F32))
        + tuple(pltpu.VMEM(x.shape, x.dtype) for x in given)
        + (pltpu.SemaphoreType.DMA((len(given),)),),
        [HBM] * len(given),
    )(*given)
    tables = tuple(jnp.asarray(x) for x in expansion())
    recv = exchange(out.reshape(devices, cap, WIDTH), fields, shards_n, 0).reshape(slots, WIDTH)
    exposure_update, back = plain(
        functools.partial(solve_kernel, cap),
        (sds((SIZE, exp_local), F32), sds((slots, LANES), F32)),
        (
            pltpu.VMEM((8 * base_of(SIZE), exp_local), F32),
            pltpu.VMEM((8, SIZE, exp_local), F32),
            pltpu.VMEM((SIZE, exp_local), F32),
            pltpu.VMEM((slots, WIDTH), F32),
        )
        + tuple(pltpu.VMEM(x.shape, x.dtype) for x in tables)
        + (pltpu.SemaphoreType.DMA((3,)),),
        [HBM] * 3,
    )(recv, *tables)
    got = exchange(back.reshape(devices, cap, LANES), fields, shards_n, 1).reshape(slots, LANES)
    late = (*given[:5], tgt, got)
    star_update, ccd_update = plain(
        functools.partial(stars_kernel, tiles, visits),
        (sds((tiles * 2, stars), F32), sds((6, NCCD), F32)),
        tuple(pltpu.VMEM(x.shape, x.dtype) for x in late) + (pltpu.SemaphoreType.DMA((7,)),),
        [HBM] * 7,
    )(*late)
    return star_update.reshape(tiles, 2, stars), exposure_update, ccd_update.T


def solution(mesh):
    in_specs = (
        P(("field", "shard"), None, None, None),
        P(("field", "shard"), None, None, None),
        P(("field", "shard"), None, None, None),
        P(("field", "shard"), None, None),
        P(("field", "shard")),
        P(("field", "shard"), None),
        P(("field", "shard"), None),
        P(),
    )
    out_specs = (P(("field", "shard"), None, None), P(None, ("field", "shard")), P())
    return jax.shard_map(shards, mesh=mesh, in_specs=in_specs, out_specs=out_specs, check_vma=False)
```

```python
import functools
import math

import jax
import jax.numpy as jnp
import numpy as np
from jax import lax
from jax.experimental import pallas as pl
from jax.experimental.pallas import tpu as pltpu
from jax.sharding import PartitionSpec as P

ORDER = 6
POLY = 28
NCCD = 189
LANES = 128
MESH = pl.DeviceIdType.MESH

STAR_DAMP = 0.1
EXPOSURE_DAMP = 1.0
DETECTOR_DAMP = 1.0

DEGREE = 2 * ORDER
BLOCK = 96
AT_GRAD = 3 * BLOCK
AT_ROW = AT_GRAD + 2 * POLY
AT_CCD = AT_ROW + 8
WIDTH = 384
AT_DET = 64
BF = jnp.bfloat16
HBM = pl.BlockSpec(memory_space=pltpu.HBM)
F32 = jnp.float32

PAIRS = [(first, total - first) for total in range(ORDER + 1) for first in range(total + 1)]
MOMENTS = [(first, second) for first in range(DEGREE + 1) for second in range(DEGREE + 1 - first)]
SPOT = {pair: at for at, pair in enumerate(MOMENTS)}
CCD_MOMENTS = [(0, 0), (1, 0), (0, 1), (2, 0), (1, 1), (0, 2)]
SIZE = 2 * POLY
TILES = SIZE // 8


def base_of(row):
    return sum(TILES - r // 8 for r in range(row))


def tile_at(row, column_tile):
    return 8 * (base_of(row) + column_tile - row // 8)


@functools.lru_cache(maxsize=None)
def expansion():
    lin = np.zeros((ORDER + 1, ORDER + 1, DEGREE + 1))
    for i in range(ORDER + 1):
        for j in range(ORDER + 1):
            one, two = np.zeros(i + 1), np.zeros(j + 1)
            one[i], two[j] = 1.0, 1.0
            prod = np.polynomial.legendre.legmul(one, two)
            lin[i, j, : len(prod)] = prod
    pair = np.zeros((POLY, POLY, BLOCK))
    for p, (i, j) in enumerate(PAIRS):
        for q, (k, l) in enumerate(PAIRS):
            scale = math.sqrt((2 * i + 1) * (2 * j + 1) * (2 * k + 1) * (2 * l + 1))
            for at, (a, b) in enumerate(MOMENTS):
                pair[p, q, at] = scale * lin[i, k, a] * lin[j, l, b]
    top, low = [], []
    for row in range(SIZE):
        for col in range(8 * (row // 8), SIZE):
            line = np.zeros(3 * BLOCK)
            kind = row // POLY + col // POLY
            line[kind * BLOCK : (kind + 1) * BLOCK] = pair[row % POLY, col % POLY]
            if row == col:
                line[kind * BLOCK + len(MOMENTS)] = EXPOSURE_DAMP
            if row < POLY:
                top.append(line[: 2 * BLOCK])
            else:
                low.append(line[2 * BLOCK :])
    return np.stack(top).astype(np.float32), np.stack(low).astype(np.float32)


def split3(x):
    high = x.astype(BF)
    rest = x - high.astype(F32)
    mid = rest.astype(BF)
    low = (rest - mid.astype(F32)).astype(BF)
    return high, mid, low


def dot(a, b):
    return jnp.dot(a, b, preferred_element_type=F32)


def dot_nt(a, b):
    return lax.dot_general(a, b, (((1,), (1,)), ((), ())), preferred_element_type=F32)


def series(value, degree_max):
    values = [jnp.ones_like(value), value]
    for degree in range(1, degree_max):
        values.append(
            (2 * degree + 1) / (degree + 1) * value * values[degree]
            - degree / (degree + 1) * values[degree - 1]
        )
    return values


def iota(shape, axis):
    return lax.broadcasted_iota(jnp.int32, shape, axis)


def star_parts(tiles, visits, off_ref, wd_ref, wc_ref, cnt_ref):
    square = iota((tiles, tiles), 0) == iota((tiles, tiles), 1)
    count = jnp.sum(jnp.where(square, cnt_ref[...].astype(F32), 0.0), axis=1, keepdims=True)
    present = (iota((tiles, LANES), 1).astype(F32) < count).astype(F32)
    weights, resid = [], []
    for k in range(visits):
        d0 = wd_ref[pl.ds(2 * k, tiles, stride=2 * visits), :]
        d1 = wd_ref[pl.ds(2 * k + 1, tiles, stride=2 * visits), :]
        corr = wc_ref[k * tiles : (k + 1) * tiles, :]
        weights.append((d0 * present, d1 * present, corr * jnp.sqrt(d0 * d1) * present))
        resid.append(
            (
                off_ref[pl.ds(2 * k, tiles, stride=2 * visits), :],
                off_ref[pl.ds(2 * k + 1, tiles, stride=2 * visits), :],
            )
        )
    hess_xx = sum(w[0] for w in weights) + STAR_DAMP
    hess_yy = sum(w[1] for w in weights) + STAR_DAMP
    hess_xy = sum(w[2] for w in weights)
    inv_det = 1.0 / (hess_xx * hess_yy - hess_xy * hess_xy)
    return weights, resid, (hess_yy * inv_det, hess_xx * inv_det, -hess_xy * inv_det)


def gradient(weights, resid):
    grad_x = sum(w[0] * r[0] + w[2] * r[1] for w, r in zip(weights, resid))
    grad_y = sum(w[2] * r[0] + w[1] * r[1] for w, r in zip(weights, resid))
    return grad_x, grad_y


def visit_row(ids, tiles, visits):
    spread = (iota((tiles, LANES), 1) % tiles == iota((tiles, LANES), 0)).astype(F32)
    rows = jnp.dot(
        ids.astype(F32), spread, precision=lax.Precision.HIGHEST, preferred_element_type=F32
    )
    keep = iota((visits, LANES), 0) == iota((visits, LANES), 1) // tiles
    return jnp.sum(jnp.where(keep, rows, 0.0), axis=0, keepdims=True)


def moments_kernel(
    tiles, visits, devices, cap, exp_local,
    uv_any, off_any, wd_any, wc_any, cnt_any, eid_any, cid_any, slot_any,
    out_ref, tgt_ref, leg_v, part,
    uv_ref, off_ref, wd_ref, wc_ref, cnt_ref, eid_ref, cid_ref, slot_ref, sems,
):
    count = tiles * visits
    copies = [
        pltpu.make_async_copy(source, target, sems.at[at])
        for at, (source, target) in enumerate(
            (
                (wd_any, wd_ref), (off_any, off_ref), (wc_any, wc_ref), (cnt_any, cnt_ref),
                (uv_any, uv_ref), (eid_any, eid_ref), (cid_any, cid_ref), (slot_any, slot_ref),
            )
        )
    ]
    for one in copies:
        one.start()
    for one in copies:
        one.wait()
    weights, resid, (inv_xx, inv_yy, inv_xy) = star_parts(
        tiles, visits, off_ref, wd_ref, wc_ref, cnt_ref
    )
    grad_x, grad_y = gradient(weights, resid)
    shift_x = inv_xx * grad_x + inv_xy * grad_y
    shift_y = inv_xy * grad_x + inv_yy * grad_y
    lists = [[] for _ in range(7)]
    for k in range(visits):
        wxx, wyy, wxy = weights[k]
        left_x, left_y = resid[k][0] - shift_x, resid[k][1] - shift_y
        prod_11 = inv_xx * wxx + inv_xy * wxy
        prod_12 = inv_xx * wxy + inv_xy * wyy
        prod_21 = inv_xy * wxx + inv_yy * wxy
        prod_22 = inv_xy * wxy + inv_yy * wyy
        for at, value in enumerate(
            (
                uv_ref[pl.ds(2 * k, tiles, stride=2 * visits), :],
                uv_ref[pl.ds(2 * k + 1, tiles, stride=2 * visits), :],
                wxx - (wxx * prod_11 + wxy * prod_21),
                wxy - (wxx * prod_12 + wxy * prod_22),
                wyy - (wxy * prod_12 + wyy * prod_22),
                wxx * left_x + wxy * left_y,
                wxy * left_x + wyy * left_y,
            )
        ):
            lists[at].append(value)
    pad = jnp.zeros((LANES - count, LANES), F32)
    cols = [jnp.concatenate(group + [pad], axis=0).T for group in lists]
    u, v = cols[0], cols[1]
    leg_u = series(u, DEGREE)
    for b, value in enumerate(series(v, DEGREE)):
        leg_v[b] = value

    def fold(value):
        return jnp.sum(value.reshape(LANES // 8, 8, LANES), axis=0)

    def put(row, value):
        part[8 * row : 8 * row + 8, :] = value

    zero = jnp.zeros((8, LANES), F32)
    for row in range(WIDTH):
        if row < AT_GRAD and row % BLOCK >= len(MOMENTS) or row >= AT_ROW:
            put(row, zero)
    for kind in range(3):
        weight = cols[2 + kind]
        for a in range(DEGREE + 1):
            scaled = weight * leg_u[a] if a else weight
            for b in range(DEGREE + 1 - a):
                value = scaled * leg_v[b] if b else scaled
                put(kind * BLOCK + SPOT[a, b], fold(value))
    for axis in range(2):
        pull = cols[5 + axis]
        for a in range(ORDER + 1):
            scaled = pull * leg_u[a] if a else pull
            for b in range(ORDER + 1 - a):
                value = scaled * leg_v[b] if b else scaled
                norm = math.sqrt((2 * a + 1) * (2 * b + 1))
                put(AT_GRAD + axis * POLY + PAIRS.index((a, b)), fold(value) * norm)
    vec = part[pl.ds(0, WIDTH, stride=8), :]
    for s in range(1, 8):
        vec = vec + part[pl.ds(s, WIDTH, stride=8), :]

    exp_id = visit_row(eid_ref[...], tiles, visits).astype(jnp.int32)
    ccd_id = visit_row(cid_ref[...], tiles, visits).astype(jnp.int32)
    groups = slot_ref.shape[0]
    pick = (iota((groups, LANES), 0) == exp_id // LANES).astype(F32)
    looked = lax.dot_general(
        slot_ref[...].astype(F32), pick, (((0,), (0,)), ((), ())),
        precision=lax.Precision.HIGHEST, preferred_element_type=F32,
    )
    inside = iota((LANES, LANES), 0) == exp_id % LANES
    place = jnp.sum(jnp.where(inside, looked, 0.0), axis=0, keepdims=True).astype(jnp.int32)
    valid = iota((1, LANES), 1) < count
    dest = jnp.where(valid, place // exp_local, -1)
    local_row = place % exp_local
    marks = (iota((devices, LANES), 0) == dest).astype(F32)
    before = (iota((LANES, LANES), 0) < iota((LANES, LANES), 1)).astype(BF)
    rank = jnp.sum(marks * dot(marks.astype(BF), before), axis=0, keepdims=True)
    target = jnp.where(valid, dest * cap + rank.astype(jnp.int32), -1)
    ccd_id = jnp.where(valid, ccd_id, -1)
    slots = devices * cap
    send = (iota((slots, LANES), 0) == target).astype(F32).astype(BF)
    seen = (iota((slots, LANES), 0) == ccd_id).astype(F32).astype(BF)
    tgt_ref[...] = jnp.where(iota((8, LANES), 0) == 0, target, ccd_id)

    vec = jnp.where(iota((WIDTH, LANES), 0) == AT_ROW, (local_row + 1).astype(F32), vec)
    out = sum(dot_nt(send, piece) for piece in split3(vec))
    picked = [vec[kind * BLOCK + SPOT[m] : kind * BLOCK + SPOT[m] + 1] for kind in range(3) for m in CCD_MOMENTS]
    for axis in range(2):
        for m in ((0, 0), (1, 0), (0, 1)):
            at = AT_GRAD + axis * POLY + PAIRS.index(m)
            picked.append(vec[at : at + 1])
    shift = AT_CCD - 2 * LANES
    ccd_vec = jnp.concatenate(
        [jnp.zeros((shift, LANES), F32)] + picked
        + [jnp.zeros((LANES - shift - len(picked), LANES), F32)], axis=0,
    )
    tail = out[:, 2 * LANES :] + sum(dot_nt(seen, piece) for piece in split3(ccd_vec))
    out_ref[...] = jnp.concatenate([out[:, : 2 * LANES], tail], axis=1)


def exchange_kernel(fields, shards_n, src_ref, dst_ref, send_sem, recv_sem, own_sem):
    devices = fields * shards_n
    me = lax.axis_index("field") * shards_n + lax.axis_index("shard")
    barrier = pltpu.get_barrier_semaphore()

    def greet(step, carry):
        peer = lax.rem(me + step, devices)
        pl.semaphore_signal(
            barrier, inc=1, device_id=(lax.div(peer, shards_n), lax.rem(peer, shards_n)), device_id_type=MESH
        )
        return carry

    lax.fori_loop(1, devices, greet, 0, unroll=True)
    own = pltpu.make_async_copy(src_ref.at[me], dst_ref.at[me], own_sem)
    own.start()
    pl.semaphore_wait(barrier, devices - 1)

    def copy(step):
        peer = lax.rem(me + step, devices)
        return pltpu.make_async_remote_copy(
            src_ref=src_ref.at[peer],
            dst_ref=dst_ref.at[me],
            send_sem=send_sem.at[step],
            recv_sem=recv_sem.at[step],
            device_id=(lax.div(peer, shards_n), lax.rem(peer, shards_n)),
            device_id_type=MESH,
        )

    def launch(step, carry):
        copy(step).start()
        return carry

    def finish(step, carry):
        copy(step).wait_send()
        origin = lax.rem(me - step + devices, devices)
        pltpu.make_async_remote_copy(
            src_ref=src_ref.at[me],
            dst_ref=dst_ref.at[origin],
            send_sem=send_sem.at[step],
            recv_sem=recv_sem.at[step],
            device_id=(lax.div(origin, shards_n), lax.rem(origin, shards_n)),
            device_id_type=MESH,
        ).wait_recv()
        return carry

    lax.fori_loop(1, devices, launch, 0, unroll=True)
    lax.fori_loop(1, devices, finish, 0, unroll=True)
    own.wait()


def exchange(values, fields, shards_n, collective_id):
    devices = fields * shards_n
    return pl.pallas_call(
        functools.partial(exchange_kernel, fields, shards_n),
        out_shape=jax.ShapeDtypeStruct(values.shape, values.dtype),
        in_specs=[pl.BlockSpec(memory_space=pltpu.HBM)],
        out_specs=pl.BlockSpec(memory_space=pltpu.HBM),
        scratch_shapes=[
            pltpu.SemaphoreType.DMA((devices,)),
            pltpu.SemaphoreType.DMA((devices,)),
            pltpu.SemaphoreType.DMA,
        ],
        compiler_params=pltpu.CompilerParams(
            collective_id=collective_id, has_side_effects=True, vmem_limit_bytes=64 * 1024 * 1024
        ),
    )(values)


def small_solve(matrix, rhs):
    size = len(rhs)
    work = [list(line) for line in matrix]
    rhs = list(rhs)
    inverse = []
    for k in range(size):
        inv = 1.0 / work[k][k]
        inverse.append(inv)
        for r in range(k + 1, size):
            coef = work[k][r] * inv
            for c in range(r, size):
                work[r][c] = work[r][c] - coef * work[k][c]
            rhs[r] = rhs[r] - coef * rhs[k]
    out = [None] * size
    for k in range(size - 1, -1, -1):
        value = rhs[k]
        for c in range(k + 1, size):
            value = value - work[k][c] * out[c]
        out[k] = value * inverse[k]
    return out


def solve_kernel(
    cap, recv_any, top_any, low_any, exp_ref, back_ref,
    mat, coefs, dinv, recv_ref, top_ref, low_ref, sems,
):
    copies = [
        pltpu.make_async_copy(source, target, sems.at[at])
        for at, (source, target) in enumerate(
            ((recv_any, recv_ref), (top_any, top_ref), (low_any, low_ref))
        )
    ]
    for one in copies:
        one.start()
    copies[0].wait()
    slots = recv_ref.shape[0]
    exp_local = exp_ref.shape[1]
    recv = recv_ref[...]
    flipped = recv.T
    rows = recv[:, AT_ROW : AT_ROW + 1]
    own = ((iota((slots, exp_local), 1) + 1).astype(F32) == rows).astype(F32).astype(BF)
    det = (iota((slots, exp_local), 1) == iota((slots, exp_local), 0) % cap).astype(F32).astype(BF)
    parts = split3(flipped)
    table = sum(dot(piece[:AT_CCD], own) for piece in parts)
    ccd = sum(dot(piece[AT_CCD:], det) for piece in parts)

    row_at = iota((AT_GRAD, exp_local), 0)
    damp = (row_at == len(MOMENTS)) | (row_at == 2 * BLOCK + len(MOMENTS))
    held = split3(jnp.where(damp, 1.0, table[:AT_GRAD]))
    split_at = top_ref.shape[0]
    copies[1].wait()
    copies[2].wait()
    for source, first, last, begin in ((top_ref, 0, 2 * BLOCK, 0), (low_ref, 2 * BLOCK, 3 * BLOCK, split_at)):
        total = None
        pieces = split3(source[...])
        for i, j in ((0, 2), (1, 1), (2, 0), (0, 1), (1, 0), (0, 0)):
            term = dot(pieces[i], held[j][first:last])
            total = term if total is None else total + term
        mat[begin : begin + source.shape[0], :] = total

    sub = iota((8, exp_local), 0)
    grad = [table[AT_GRAD + 8 * t : AT_GRAD + 8 * t + 8] for t in range(TILES)]
    for kb in range(TILES):
        block = [
            [mat[tile_at(8 * kb + r, jt) : tile_at(8 * kb + r, jt) + 8, :] for jt in range(kb, TILES)]
            for r in range(8)
        ]
        for r in range(8):
            inv = 1.0 / block[r][0][r : r + 1]
            dinv[8 * kb + r : 8 * kb + r + 1, :] = inv
            scaled = [tile * inv for tile in block[r]]
            for at, tile in enumerate(scaled):
                coefs[r, 8 * (kb + at) : 8 * (kb + at) + 8, :] = tile
            for r2 in range(r + 1, 8):
                coef = scaled[0][r2 : r2 + 1]
                block[r2] = [x - coef * y for x, y in zip(block[r2], block[r])]
            step = grad[kb][r : r + 1]
            grad[kb] = grad[kb] - jnp.where(sub > r, scaled[0] * step, 0.0)
            for at in range(1, TILES - kb):
                grad[kb + at] = grad[kb + at] - scaled[at] * step
        for r in range(8):
            for at, tile in enumerate(block[r]):
                start = tile_at(8 * kb + r, kb + at)
                mat[start : start + 8, :] = tile
        for jt in range(kb + 1, TILES):
            for row in range(8 * kb + 8, 8 * jt + 8):
                start = tile_at(row, jt)
                value = mat[start : start + 8, :]
                for r in range(8):
                    value = value - coefs[r, row : row + 1, :] * block[r][jt - kb]
                mat[start : start + 8, :] = value

    answer = [None] * TILES
    for kb in range(TILES - 1, -1, -1):
        rest, inner = [], []
        for r in range(8):
            line = grad[kb][r : r + 1]
            if kb + 1 < TILES:
                total = None
                for jt in range(kb + 1, TILES):
                    start = tile_at(8 * kb + r, jt)
                    term = mat[start : start + 8, :] * answer[jt]
                    total = term if total is None else total + term
                line = line - jnp.sum(total, axis=0, keepdims=True)
            rest.append(line)
            start = tile_at(8 * kb + r, kb)
            inner.append(mat[start : start + 8, :])
        found = [None] * 8
        for r in range(7, -1, -1):
            found[r] = rest[r] * dinv[8 * kb + r : 8 * kb + r + 1, :]
            for r2 in range(r):
                rest[r2] = rest[r2] - inner[r2][r : r + 1] * found[r]
        answer[kb] = jnp.concatenate(found, axis=0)
    solved = jnp.concatenate(answer, axis=0)
    exp_ref[...] = solved

    lines = [ccd[i : i + 1] for i in range(24)]
    grams = []
    for kind in range(3):
        m00, m10, m01, m20, m11, m02 = lines[6 * kind : 6 * kind + 6]
        uu = (2.0 * m20 + m00) * (1.0 / 3.0)
        vv = (2.0 * m02 + m00) * (1.0 / 3.0)
        grams.append([[m00, m10, m01], [m10, uu, m11], [m01, m11, vv]])
    root = 1.0 / math.sqrt(3.0)
    rhs = [lines[18], lines[19] * root, lines[20] * root, lines[21], lines[22] * root, lines[23] * root]
    matrix = [
        [grams[i // 3 + j // 3][i % 3][j % 3] + (DETECTOR_DAMP if i == j else 0.0) for j in range(6)]
        for i in range(6)
    ]
    det_update = small_solve(matrix, rhs)

    exp_rows = jnp.concatenate([solved, jnp.zeros((LANES - SIZE, exp_local), F32)], axis=0)
    det_rows = jnp.concatenate(
        [jnp.zeros((AT_DET, exp_local), F32)] + det_update
        + [jnp.zeros((LANES - AT_DET - 6, exp_local), F32)], axis=0,
    )
    back = sum(dot_nt(own, piece) for piece in split3(exp_rows))
    back_ref[...] = back + sum(dot_nt(det, piece) for piece in split3(det_rows))


def stars_kernel(
    tiles, visits, *refs
):
    sources, (star_ref, ccd_ref), targets, sems = refs[:7], refs[7:9], refs[9:16], refs[16]
    uv_ref, off_ref, wd_ref, wc_ref, cnt_ref, tgt_ref, back_ref = targets
    copies = [
        pltpu.make_async_copy(source, target, sems.at[at])
        for at, (source, target) in enumerate(zip(sources, targets))
    ]
    for one in reversed(copies):
        one.start()
    for one in reversed(copies):
        one.wait()
    back = back_ref[...]
    slots = back.shape[0]
    ccd_ref[...] = back.T[AT_DET : AT_DET + 6, :NCCD]
    pieces = split3(back)

    def take(row):
        wide = jnp.broadcast_to(tgt_ref[row : row + 1, :].astype(F32), (LANES, LANES)).T
        wide = jnp.concatenate([wide] * (slots // LANES), axis=1)
        chosen = (iota((LANES, slots), 1).astype(F32) == wide).astype(F32).astype(BF)
        return sum(dot(chosen, piece) for piece in pieces)

    exp_coef = take(0)
    det_coef = take(1)
    weights, resid, (inv_xx, inv_yy, inv_xy) = star_parts(
        tiles, visits, off_ref, wd_ref, wc_ref, cnt_ref
    )
    root = 1.0 / math.sqrt(3.0)
    moved = []
    for k in range(visits):
        u = uv_ref[pl.ds(2 * k, tiles, stride=2 * visits), :]
        v = uv_ref[pl.ds(2 * k + 1, tiles, stride=2 * visits), :]
        leg_u = [x * math.sqrt(2 * n + 1) for n, x in enumerate(series(u, ORDER))]
        leg_v = [x * math.sqrt(2 * n + 1) for n, x in enumerate(series(v, ORDER))]
        lines = slice(k * tiles, (k + 1) * tiles)
        model = []
        for axis in range(2):
            extra = {(0, 0): (0, 1.0), (1, 0): (1, root), (0, 1): (2, root)}
            total = None
            for a in range(ORDER + 1):
                inner = None
                for b in range(ORDER + 1 - a):
                    at = axis * POLY + PAIRS.index((a, b))
                    coef = exp_coef[lines, at : at + 1]
                    if (a, b) in extra:
                        where, scale = extra[a, b]
                        where += AT_DET + 3 * axis
                        coef = coef + det_coef[lines, where : where + 1] * scale
                    term = coef * leg_v[b] if b else jnp.broadcast_to(coef, u.shape)
                    inner = term if inner is None else inner + term
                term = leg_u[a] * inner if a else inner
                total = term if total is None else total + term
            model.append(total)
        moved.append((resid[k][0] - model[0], resid[k][1] - model[1]))
    grad_x, grad_y = gradient(weights, moved)
    star_ref[pl.ds(0, tiles, stride=2), :] = inv_xx * grad_x + inv_xy * grad_y
    star_ref[pl.ds(1, tiles, stride=2), :] = inv_xy * grad_x + inv_yy * grad_y


def plain(kernel, out_shape, scratch=(), in_place=None):
    extra = {} if in_place is None else {"in_specs": in_place}
    return pl.pallas_call(
        kernel,
        out_shape=out_shape,
        **extra,
        scratch_shapes=list(scratch),
        compiler_params=pltpu.CompilerParams(vmem_limit_bytes=64 * 1024 * 1024),
    )


def shards(focal_uv, offsets, w_diag, w_corr, star_count, exposure_ids, ccd_ids, exp_slot):
    shards_n = lax.axis_size("shard")
    fields = lax.axis_size("field")
    devices = shards_n * fields
    tiles, visits, _, stars = offsets.shape
    cap = 2 * tiles * visits // (3 * shards_n)
    slots = devices * cap
    exp_local = exp_slot.shape[0] // devices
    assert slots >= NCCD and slots % LANES == 0 and tiles * visits <= LANES and stars == LANES
    sds = jax.ShapeDtypeStruct
    uv = focal_uv.reshape(tiles * visits * 2, stars)
    off = offsets.reshape(tiles * visits * 2, stars)
    wd = w_diag.reshape(tiles * visits * 2, stars)
    wc = w_corr.transpose(1, 0, 2).reshape(tiles * visits, stars)
    cnt = star_count.reshape(1, tiles)
    given = (uv, off, wd, wc, cnt, exposure_ids.T, ccd_ids.T, exp_slot.reshape(-1, LANES))
    out, tgt = plain(
        functools.partial(moments_kernel, tiles, visits, devices, cap, exp_local),
        (sds((slots, WIDTH), F32), sds((8, LANES), jnp.int32)),
        (pltpu.VMEM((DEGREE + 1, stars, LANES), F32), pltpu.VMEM((8 * WIDTH, LANES), F32))
        + tuple(pltpu.VMEM(x.shape, x.dtype) for x in given)
        + (pltpu.SemaphoreType.DMA((len(given),)),),
        [HBM] * len(given),
    )(*given)
    tables = tuple(jnp.asarray(x) for x in expansion())
    recv = exchange(out.reshape(devices, cap, WIDTH), fields, shards_n, 0).reshape(slots, WIDTH)
    exposure_update, back = plain(
        functools.partial(solve_kernel, cap),
        (sds((SIZE, exp_local), F32), sds((slots, LANES), F32)),
        (
            pltpu.VMEM((8 * base_of(SIZE), exp_local), F32),
            pltpu.VMEM((8, SIZE, exp_local), F32),
            pltpu.VMEM((SIZE, exp_local), F32),
            pltpu.VMEM((slots, WIDTH), F32),
        )
        + tuple(pltpu.VMEM(x.shape, x.dtype) for x in tables)
        + (pltpu.SemaphoreType.DMA((3,)),),
        [HBM] * 3,
    )(recv, *tables)
    got = exchange(back.reshape(devices, cap, LANES), fields, shards_n, 1).reshape(slots, LANES)
    late = (*given[:5], tgt, got)
    star_update, ccd_update = plain(
        functools.partial(stars_kernel, tiles, visits),
        (sds((tiles * 2, stars), F32), sds((6, NCCD), F32)),
        tuple(pltpu.VMEM(x.shape, x.dtype) for x in late) + (pltpu.SemaphoreType.DMA((7,)),),
        [HBM] * 7,
    )(*late)
    return star_update.reshape(tiles, 2, stars), exposure_update, ccd_update.T


def solution(mesh):
    in_specs = (
        P(("field", "shard"), None, None, None),
        P(("field", "shard"), None, None, None),
        P(("field", "shard"), None, None, None),
        P(("field", "shard"), None, None),
        P(("field", "shard")),
        P(("field", "shard"), None),
        P(("field", "shard"), None),
        P(),
    )
    out_specs = (P(("field", "shard"), None, None), P(None, ("field", "shard")), P())
    return jax.shard_map(shards, mesh=mesh, in_specs=in_specs, out_specs=out_specs, check_vma=False)
```
